32 devices in a mesh: scene: 2 (over y), lines: 16 (over z, x, core).
Axes of the slice: x: 2, y: 2, z: 4, core: 2. Of those that a mesh axis runs over, the one named last changes fastest.
Arguments:
- pixels: bfloat16 [1024, 128, 256], P(('scene', 'lines')), parts along dimension 0, may hold values from -100 to 100
- scene_lines: int32 [2], P('scene'), parts along dimension 0, may hold values from 385 to 512
- scene_cols: int32 [2], P('scene'), parts along dimension 0, may hold values from 33 to 128
Outputs:
- anomaly: float32 [1024, 128], P(('scene', 'lines')), parts along dimension 0
The draws below stay inside these ranges and needn't reach their ends.
There are 2 independent parts, one for each index of `scene`. The reference program is written for one: setup_inputs(seed, part) draws one part's arguments, and reference() takes and returns one part's arrays. A program takes and returns all parts, laid end to end along the dimension named above; each array names one. Nothing has to cross between parts.
Inputs may be any that keep to these rules, and one draw needn't show every extreme that they name: The scene occupies the first scene_lines lines of the array. The scene occupies the first scene_cols columns of every line.
All inputs are finite; a program needn't handle non-finite values.
Results may differ from the reference program's by a relative error of at most 0.0003.
Values may be sent and summed in bfloat16 or wider, within the bound.
A program may use at most 64 MiB of HBM per device.

```python
import math
import jax
import jax.numpy as jnp
from jax import lax

BANDS = 256
COLS = 128
LINES_DEV = 32
OUTER = 32
GUARD = 4
LINES = 512


def smooth_background(key):
    keys = jax.random.split(jax.random.fold_in(key, 29), 4)
    line_period = jnp.exp(jax.random.uniform(keys[0], (4,), jnp.float32, math.log(8.0 * OUTER), math.log(32.0 * OUTER)))
    col_period = jnp.exp(jax.random.uniform(keys[1], (4,), jnp.float32, math.log(2.0 * COLS), math.log(4.0 * COLS)))
    phases = jax.random.uniform(keys[2], (2, 4), jnp.float32, 0.0, 2.0 * math.pi)
    weights = 0.375 * jax.random.uniform(keys[3], (4, BANDS), jnp.float32, -1.0, 1.0)
    line_pos = jnp.arange(LINES, dtype=jnp.float32)
    col_pos = jnp.arange(COLS, dtype=jnp.float32)
    line_wave = jnp.cos(2.0 * math.pi * line_pos[:, None] / line_period[None, :] + phases[0][None, :])
    col_wave = jnp.cos(2.0 * math.pi * col_pos[:, None] / col_period[None, :] + phases[1][None, :])
    return jnp.einsum('lk,ck,kb->lcb', line_wave, col_wave, weights, precision=lax.Precision.HIGHEST)


def draw_pixels(key, part):
    keys = jax.random.split(jax.random.fold_in(key, 11), 7)
    band_scale = jnp.exp(jax.random.uniform(keys[0], (BANDS,), jnp.float32, jnp.log(0.3), jnp.log(3.0)))
    position = jnp.arange(LINES, dtype=jnp.float32) / max(LINES - 1, 1)
    ramp = 1.0 + 2.0 * position
    background = smooth_background(keys[4]) * ramp[:, None, None] * band_scale
    level_sign = jnp.where(jax.random.uniform(keys[5], (BANDS,), jnp.float32) < 0.5, -1.0, 1.0)
    level = level_sign * jax.random.uniform(keys[6], (BANDS,), jnp.float32, 0.5, 1.5) * band_scale
    base = jax.random.truncated_normal(keys[1], -4.0, 4.0, (LINES, COLS, BANDS), jnp.float32)
    values = base * ramp[:, None, None] * band_scale + background + 1.5 * ramp[:, None, None] * level
    return values.astype(jnp.bfloat16)


def setup_inputs(seed: int = 0, part: int = 0) -> dict:
    key_list = jax.random.split(jax.random.key(seed), 4)
    part_splits = jax.random.split(jax.random.fold_in(key_list[3], part), 4)
    pixels = draw_pixels(jax.random.fold_in(jax.random.fold_in(key_list[3], part), 71), part)
    scene_lines = jax.random.randint(part_splits[1], (1,), LINES - 4 * LINES_DEV + 1, LINES + 1).astype(jnp.int32)
    scene_cols = jax.random.randint(part_splits[2], (1,), COLS // 4 + 1, COLS + 1).astype(jnp.int32)
    return {"pixels": pixels, "scene_lines": scene_lines, "scene_cols": scene_cols}


def window_matrix(rows_out, rows_in, offset, radius):
    row_index = lax.broadcasted_iota(jnp.int32, (rows_out, rows_in), 0)
    col_index = lax.broadcasted_iota(jnp.int32, (rows_out, rows_in), 1)
    return jnp.abs(col_index - offset - row_index) <= radius

def cycle_part(source, offset, lines_here):
    lines_in, cols_here, band_count = source.shape
    flat_source = source.reshape(lines_in, cols_here * band_count)
    outer_lines = window_matrix(lines_here, lines_in, offset, OUTER).astype(jnp.bfloat16)
    guard_lines = window_matrix(lines_here, lines_in, offset, GUARD).astype(jnp.bfloat16)
    outer_sum = jnp.dot(outer_lines.astype(jnp.float32), flat_source.astype(jnp.float32), preferred_element_type=jnp.float32).reshape(lines_here, cols_here, band_count)
    guard_sum = jnp.dot(guard_lines.astype(jnp.float32), flat_source.astype(jnp.float32), preferred_element_type=jnp.float32).reshape(lines_here, cols_here, band_count)
    outer_cols = window_matrix(cols_here, cols_here, 0, OUTER).astype(jnp.float32)
    guard_cols = window_matrix(cols_here, cols_here, 0, GUARD).astype(jnp.float32)
    first = jnp.einsum('cd,ldb->lcb', outer_cols, outer_sum, precision=lax.Precision.HIGHEST)
    second = jnp.einsum('cd,ldb->lcb', guard_cols, guard_sum, precision=lax.Precision.HIGHEST)
    return first - second

def cycle_counts(first_line, last_line, last_col, lines_here, cols_here):
    ext_line = first_line - OUTER + jnp.arange(lines_here + 2 * OUTER, dtype=jnp.int32)
    line_valid = ((ext_line >= 0) & (ext_line < last_line)).astype(jnp.float32)
    col_valid = (jnp.arange(cols_here, dtype=jnp.int32) < last_col).astype(jnp.float32)
    span = lines_here + 2 * OUTER
    outer_l = jnp.sum(jnp.where(window_matrix(lines_here, span, OUTER, OUTER), line_valid[None, :], 0.0), axis=1)
    guard_l = jnp.sum(jnp.where(window_matrix(lines_here, span, OUTER, GUARD), line_valid[None, :], 0.0), axis=1)
    outer_c = jnp.sum(jnp.where(window_matrix(cols_here, cols_here, 0, OUTER), col_valid[None, :], 0.0), axis=1)
    guard_c = jnp.sum(jnp.where(window_matrix(cols_here, cols_here, 0, GUARD), col_valid[None, :], 0.0), axis=1)
    return outer_l[:, None] * outer_c[None, :] - guard_l[:, None] * guard_c[None, :]

def reference(pixels, scene_lines, scene_cols):
    lines_all, cols_here, band_count = pixels.shape
    last_line = scene_lines[0]
    last_col = scene_cols[0]
    line_index = jnp.arange(lines_all, dtype=jnp.int32)
    col_index = jnp.arange(cols_here, dtype=jnp.int32)
    valid_mask = (line_index < last_line)[:, None] & (col_index < last_col)[None, :]
    masked = jnp.where(valid_mask[:, :, None], pixels, jnp.zeros((), pixels.dtype))
    pixel_total = (last_line * last_col).astype(jnp.float32)
    band_sums = jnp.sum(masked, axis=(0, 1), dtype=jnp.float32)
    spectral_mean = band_sums / pixel_total
    block_total = LINES // LINES_DEV

    def add_block(running, block_index):
        block_pixels = lax.dynamic_slice_in_dim(masked, (block_index * LINES_DEV).astype(jnp.int32), LINES_DEV, 0)
        block_valid = lax.dynamic_slice_in_dim(valid_mask, (block_index * LINES_DEV).astype(jnp.int32), LINES_DEV, 0)
        centered = jnp.where(block_valid.reshape(-1, 1), block_pixels.reshape(-1, band_count).astype(jnp.float32) - spectral_mean, 0.0)
        product = lax.dot_general(centered.astype(jnp.float32), centered.astype(jnp.float32), (((0,), (0,)), ((), ())), precision=lax.Precision.HIGHEST, preferred_element_type=jnp.float32)
        return (running + product, None)
    gram, _ = lax.scan(add_block, jnp.zeros((band_count, band_count), jnp.float32), jnp.arange(block_total, dtype=jnp.int32))
    covariance = gram / (pixel_total - 1.0)
    factor = jnp.linalg.cholesky(covariance)
    whiten = lax.linalg.triangular_solve(factor, jnp.eye(band_count, dtype=jnp.float32), left_side=True, lower=True)
    padded = jnp.pad(masked, ((OUTER, OUTER), (0, 0), (0, 0)))

    def block_score(block_index):
        first_line = (block_index * LINES_DEV).astype(jnp.int32)
        extended = lax.dynamic_slice_in_dim(padded, first_line, LINES_DEV + 2 * OUTER, 0)
        cycle_sum = cycle_part(extended, OUTER, LINES_DEV)
        counts = jnp.maximum(cycle_counts(first_line, last_line, last_col, LINES_DEV, cols_here), 1.0)
        local_mean = cycle_sum / counts[:, :, None]
        block_pixels = lax.dynamic_slice_in_dim(pixels, first_line, LINES_DEV, 0)
        deviation = (block_pixels.astype(jnp.float32) - local_mean).reshape(-1, band_count)
        whitened = lax.dot_general(deviation.astype(jnp.float32), whiten.astype(jnp.float32), (((1,), (1,)), ((), ())), precision=lax.Precision.HIGHEST, preferred_element_type=jnp.float32)
        anomaly = jnp.sum(whitened * whitened, axis=1).reshape(LINES_DEV, cols_here) / band_count
        block_valid = lax.dynamic_slice_in_dim(valid_mask, first_line, LINES_DEV, 0)
        return jnp.where(block_valid, anomaly, 0.0)
    scores = lax.map(block_score, jnp.arange(block_total, dtype=jnp.int32))
    return scores.reshape(lines_all, cols_here)
```

```python
import functools

import jax
import jax.numpy as jnp
from jax import lax
from jax.experimental import pallas as pl
from jax.experimental.pallas import tpu as pltpu
from jax.sharding import PartitionSpec as P

OUTER = 32
GUARD = 4
SLAB = 32
HIGHEST = lax.Precision.HIGHEST
MESH = pl.DeviceIdType.MESH
BF16 = jnp.bfloat16
F32 = jnp.float32
TN = (((0,), (0,)), ((), ()))
NT = (((1,), (1,)), ((), ()))


def iota(shape, dim):
    return lax.broadcasted_iota(jnp.int32, shape, dim)


def split(value):
    high = value.astype(BF16)
    return high, (value - high.astype(F32)).astype(BF16)


def gram_kernel(info, x_ref, out_ref, gram, sums):
    lines, cols, bands = x_ref.shape
    first, last_line, last_col = info[0], info[1], info[2]
    col_ok = iota((cols, bands), 0) < last_col
    gram[...] = jnp.zeros_like(gram)
    sums[...] = jnp.zeros_like(sums)
    step = 4

    def add(i, _):
        rows = []
        for j in range(step):
            line = i * step + j
            ok = col_ok & (first + line < last_line)
            rows.append(jnp.where(ok, x_ref[line].astype(F32), 0.0).astype(BF16))
        block = jnp.concatenate(rows, axis=0)
        gram[...] += lax.dot_general(block, block, TN, preferred_element_type=F32)
        ones = jnp.ones((8, step * cols), BF16)
        sums[...] += jnp.dot(ones, block, preferred_element_type=F32)
        return 0

    lax.fori_loop(0, lines // step, add, 0)
    h = bands // 2
    out_ref[0:h] = gram[:h, :h]
    out_ref[h : 2 * h] = gram[:h, h:]
    out_ref[2 * h : 3 * h] = gram[h:, h:]
    out_ref[3 * h :] = jnp.zeros((h, h), F32)
    out_ref[3 * h : 3 * h + 8] = sums[:, :h]
    out_ref[3 * h + 8 : 3 * h + 16] = sums[:, h:]


def reduce_kernel(n, g_ref, out_ref, recv, s1, r1, s2, r2):
    me = lax.axis_index("lines")
    bar = pltpu.get_barrier_semaphore()

    def greet(d, _):
        pl.semaphore_signal(bar, inc=1, device_id={"lines": lax.rem(me + d, n)}, device_id_type=MESH)
        return 0

    lax.fori_loop(1, n, greet, 0)
    pl.semaphore_wait(bar, n - 1)

    def scatter(d):
        peer = lax.rem(me + d, n)
        return pltpu.make_async_remote_copy(
            src_ref=g_ref.at[peer], dst_ref=recv.at[me], send_sem=s1.at[d], recv_sem=r1.at[d],
            device_id={"lines": peer}, device_id_type=MESH)

    def gather(d):
        peer = lax.rem(me + d, n)
        return pltpu.make_async_remote_copy(
            src_ref=out_ref.at[me], dst_ref=out_ref.at[me], send_sem=s2.at[d], recv_sem=r2.at[d],
            device_id={"lines": peer}, device_id_type=MESH)

    def start1(d, _):
        scatter(d).start()
        return 0

    lax.fori_loop(1, n, start1, 0)

    def take(d, total):
        source = lax.rem(me + n - d, n)
        pltpu.make_async_remote_copy(
            src_ref=g_ref.at[source], dst_ref=recv.at[source], send_sem=s1.at[d], recv_sem=r1.at[d],
            device_id={"lines": source}, device_id_type=MESH).wait_recv()
        return total + recv[source]

    out_ref[me] = lax.fori_loop(1, n, take, g_ref[me])

    def start2(d, _):
        gather(d).start()
        return 0

    lax.fori_loop(1, n, start2, 0)

    def finish(d, _):
        source = lax.rem(me + n - d, n)
        pltpu.make_async_remote_copy(
            src_ref=out_ref.at[source], dst_ref=out_ref.at[source], send_sem=s2.at[d], recv_sem=r2.at[d],
            device_id={"lines": source}, device_id_type=MESH).wait_recv()
        scatter(d).wait_send()
        gather(d).wait_send()
        return 0

    lax.fori_loop(1, n, finish, 0)


def whiten_kernel(info, g_ref, high_ref, low_ref, mat):
    h = g_ref.shape[1]
    bands = 2 * h
    total = (info[1] * info[2]).astype(F32)
    sums = jnp.concatenate([g_ref[3 * h : 3 * h + 8], g_ref[3 * h + 8 : 3 * h + 16]], axis=1)
    sums = jnp.where(iota((8, bands), 0) == 0, sums, 0.0)
    outer = lax.dot_general(sums, sums, TN, precision=HIGHEST, preferred_element_type=F32)
    scale = total - 1.0
    mat[:h, :h] = (g_ref[0:h] - outer[:h, :h] / total) / scale
    mat[:h, h:] = (g_ref[h : 2 * h] - outer[:h, h:] / total) / scale
    mat[h:, h:] = (g_ref[2 * h : 3 * h] - outer[h:, h:] / total) / scale
    mat[h:, :h] = jnp.zeros((h, h), F32)
    lane = iota((SLAB, bands), 1)
    row = iota((SLAB, bands), 0)
    for base in range(0, bands, SLAB):
        slab = mat[base : base + SLAB, :]
        pivots = jnp.ones((SLAB, bands), F32)
        for j in range(SLAB):
            k = base + j
            column = jnp.broadcast_to(slab[:, k : k + 1], (SLAB, bands))
            pivot = jnp.broadcast_to(column[j : j + 1, :], (SLAB, bands))
            pivots = jnp.where(row == j, pivot, pivots)
            factor = jnp.where(row > j, column / pivot, 0.0)
            line = jnp.broadcast_to(slab[j : j + 1, :], (SLAB, bands))
            line = jnp.where(lane == k, 1.0, line)
            slab = jnp.where((lane == k) & (row > j), 0.0, slab) - factor * line
        inside = (lane >= base) & (lane < base + SLAB)
        unit = jnp.where(lane == base + row, 1.0, jnp.where(inside & (lane > base + row), 0.0, slab))
        below = jnp.where(lane < base + SLAB, unit, 0.0)
        high, low = split(below * lax.rsqrt(pivots))
        high_ref[base : base + SLAB, :] = high
        low_ref[base : base + SLAB, :] = low
        rest = bands - base - SLAB
        if rest:
            update = lax.dot_general(
                slab, unit / pivots, TN, precision=HIGHEST, preferred_element_type=F32)
            old = mat[base + SLAB :, :]
            wide = iota((rest, bands), 1)
            cleared = jnp.where((wide >= base) & (wide < base + SLAB), 0.0, old)
            mat[base + SLAB :, :] = cleared - update[base + SLAB :, :]


def score_kernel(info, x_ref, before_ref, after_ref, high_ref, low_ref, out_ref, ext, outer, guard):
    lines, cols, bands = x_ref.shape
    first, last_line, last_col = info[0], info[1], info[2]
    col_ok = iota((cols, bands), 0) < last_col

    def mask(i, _):
        for part, ref in enumerate((before_ref, x_ref, after_ref)):
            line = first + (part - 1) * lines + i
            ok = col_ok & (line >= 0) & (line < last_line)
            ext[part * lines + i] = jnp.where(ok, ref[i].astype(F32), 0.0).astype(BF16)
        return 0

    lax.fori_loop(0, lines, mask, 0)

    def total(lo, hi):
        def add(i, acc):
            return acc + ext[i].astype(F32)
        return lax.fori_loop(lo, hi, add, jnp.zeros((cols, bands), F32))

    outer[...] = total(lines - OUTER, lines + OUTER)
    guard[...] = total(lines - GUARD, lines + GUARD)
    gap = jnp.abs(iota((cols, cols), 0) - iota((cols, cols), 1))
    near = jnp.where(gap <= OUTER, 1.0, 0.0).astype(BF16)
    close = jnp.where(gap <= GUARD, -1.0, 0.0).astype(BF16)
    windows = jnp.concatenate([near, near, close, close], axis=1)
    col = iota((cols, bands), 0)

    def span(place, end, radius):
        return jnp.maximum(jnp.minimum(place + radius, end - 1) - jnp.maximum(place - radius, 0) + 1, 0)

    outer_cols = span(col, last_col, OUTER).astype(F32)
    guard_cols = span(col, last_col, GUARD).astype(F32)
    step = 2

    def score(i, _):
        highs, lows = [], []
        for j in range(step):
            line = i * step + j
            at = lines + line
            wide = outer[...] + ext[at + OUTER].astype(F32)
            tight = guard[...] + ext[at + GUARD].astype(F32)
            stack = jnp.concatenate(split(wide) + split(tight), axis=0)
            outer[...] = wide - ext[at - OUTER].astype(F32)
            guard[...] = tight - ext[at - GUARD].astype(F32)
            cycle = jnp.dot(windows, stack, preferred_element_type=F32)
            place = first + line
            count = (span(place, last_line, OUTER).astype(F32) * outer_cols
                     - span(place, last_line, GUARD).astype(F32) * guard_cols)
            deviation = x_ref[line].astype(F32) - cycle / jnp.maximum(count, 1.0)
            high, low = split(deviation)
            highs.append(high)
            lows.append(low)
        high = jnp.concatenate(highs, axis=0)
        low = jnp.concatenate(lows, axis=0)
        white = lax.dot_general(high_ref[...], high, NT, preferred_element_type=F32)
        white += lax.dot_general(high_ref[...], low, NT, preferred_element_type=F32)
        white += lax.dot_general(low_ref[...], high, NT, preferred_element_type=F32)
        power = jnp.sum(white * white, axis=0, keepdims=True) / bands
        for j in range(step):
            line = i * step + j
            ok = (iota((1, cols), 1) < last_col) & (first + line < last_line)
            out_ref[pl.ds(line, 1), :] = jnp.where(ok, power[:, j * cols : (j + 1) * cols], 0.0)
        return 0

    lax.fori_loop(0, lines // step, score, 0)


VMEM = pl.BlockSpec(memory_space=pltpu.VMEM)
SMEM = pl.BlockSpec(memory_space=pltpu.SMEM)


def call(kernel, out_shape, specs, scratch, limit, flops, moved, **params):
    return pl.pallas_call(
        kernel, out_shape=out_shape, in_specs=specs,
        out_specs=jax.tree.map(lambda _: VMEM, out_shape), scratch_shapes=scratch,
        compiler_params=pltpu.CompilerParams(vmem_limit_bytes=limit << 20, **params),
        cost_estimate=pl.CostEstimate(flops=flops, bytes_accessed=moved, transcendentals=0))


def body(pixels, scene_lines, scene_cols):
    lines, cols, bands = pixels.shape
    n = lax.axis_size("lines")
    first = lax.axis_index("lines") * lines
    info = jnp.concatenate([first[None].astype(jnp.int32), scene_lines, scene_cols])
    before = lax.ppermute(pixels, "lines", [(i, i + 1) for i in range(n - 1)])
    after = lax.ppermute(pixels, "lines", [(i + 1, i) for i in range(n - 1)])
    half = bands // 2
    gram = call(
        gram_kernel, jax.ShapeDtypeStruct((4 * half, half), F32), [SMEM, VMEM],
        [pltpu.VMEM((bands, bands), F32), pltpu.VMEM((8, bands), F32)], 16,
        4000000000, pixels.size * 2)(info, pixels)
    gram = gram.reshape(n, 4 * half // n, half)
    sems = [pltpu.SemaphoreType.DMA((n,))] * 4
    gram = call(
        functools.partial(reduce_kernel, n), jax.ShapeDtypeStruct(gram.shape, F32), [VMEM],
        [pltpu.VMEM(gram.shape, F32)] + sems, 16, 4000000000, 40000000,
        collective_id=0, has_side_effects=True)(gram)
    gram = gram.reshape(4 * half, half)
    shape = jax.ShapeDtypeStruct((bands, bands), BF16)
    high, low = call(
        whiten_kernel, [shape, shape], [SMEM, VMEM], [pltpu.VMEM((bands, bands), F32)], 16,
        10000000000, 60000000)(info, gram)
    return call(
        score_kernel, jax.ShapeDtypeStruct((lines, cols), F32), [SMEM] + [VMEM] * 5,
        [pltpu.VMEM((lines + 2 * OUTER, cols, bands), BF16)] + [pltpu.VMEM((cols, bands), F32)] * 2, 40,
        8000000000, 8000000)(info, pixels, before, after, high, low)


def solution(mesh):
    in_specs = (P(("scene", "lines"), None, None), P("scene"), P("scene"))
    out_specs = P(("scene", "lines"), None)
    return jax.shard_map(body, mesh=mesh, in_specs=in_specs, out_specs=out_specs, check_vma=False)
```

```python
import functools

import jax
import jax.numpy as jnp
from jax import lax
from jax.experimental import pallas as pl
from jax.experimental.pallas import tpu as pltpu
from jax.sharding import PartitionSpec as P

OUTER = 32
GUARD = 4
SLAB = 32
HIGHEST = lax.Precision.HIGHEST
MESH = pl.DeviceIdType.MESH
BF16 = jnp.bfloat16
F32 = jnp.float32
TN = (((0,), (0,)), ((), ()))
NT = (((1,), (1,)), ((), ()))


def iota(shape, dim):
    return lax.broadcasted_iota(jnp.int32, shape, dim)


def split(value):
    high = value.astype(BF16)
    return high, (value - high.astype(F32)).astype(BF16)


def gram_kernel(info, x_ref, out_ref, gram, sums):
    lines, cols, bands = x_ref.shape
    first, last_line, last_col = info[0], info[1], info[2]
    col_ok = iota((cols, bands), 0) < last_col
    gram[...] = jnp.zeros_like(gram)
    sums[...] = jnp.zeros_like(sums)
    step = 4

    def add(i, _):
        rows = []
        for j in range(step):
            line = i * step + j
            ok = col_ok & (first + line < last_line)
            rows.append(jnp.where(ok, x_ref[line].astype(F32), 0.0).astype(BF16))
        block = jnp.concatenate(rows, axis=0)
        gram[...] += lax.dot_general(block, block, TN, preferred_element_type=F32)
        ones = jnp.ones((8, step * cols), BF16)
        sums[...] += jnp.dot(ones, block, preferred_element_type=F32)
        return 0

    lax.fori_loop(0, lines // step, add, 0)
    h = bands // 2
    out_ref[0:h] = gram[:h, :h]
    out_ref[h : 2 * h] = gram[:h, h:]
    out_ref[2 * h : 3 * h] = gram[h:, h:]
    out_ref[3 * h :] = jnp.zeros((h, h), F32)
    out_ref[3 * h : 3 * h + 8] = sums[:, :h]
    out_ref[3 * h + 8 : 3 * h + 16] = sums[:, h:]


def reduce_kernel(n, g_ref, out_ref, recv, s1, r1, s2, r2):
    me = lax.axis_index("lines")
    bar = pltpu.get_barrier_semaphore()

    def greet(d, _):
        pl.semaphore_signal(bar, inc=1, device_id={"lines": lax.rem(me + d, n)}, device_id_type=MESH)
        return 0

    lax.fori_loop(1, n, greet, 0)
    pl.semaphore_wait(bar, n - 1)

    def scatter(d):
        peer = lax.rem(me + d, n)
        return pltpu.make_async_remote_copy(
            src_ref=g_ref.at[peer], dst_ref=recv.at[me], send_sem=s1.at[d], recv_sem=r1.at[d],
            device_id={"lines": peer}, device_id_type=MESH)

    def gather(d):
        peer = lax.rem(me + d, n)
        return pltpu.make_async_remote_copy(
            src_ref=out_ref.at[me], dst_ref=out_ref.at[me], send_sem=s2.at[d], recv_sem=r2.at[d],
            device_id={"lines": peer}, device_id_type=MESH)

    def start1(d, _):
        scatter(d).start()
        return 0

    lax.fori_loop(1, n, start1, 0)

    def take(d, total):
        source = lax.rem(me + n - d, n)
        pltpu.make_async_remote_copy(
            src_ref=g_ref.at[source], dst_ref=recv.at[source], send_sem=s1.at[d], recv_sem=r1.at[d],
            device_id={"lines": source}, device_id_type=MESH).wait_recv()
        return total + recv[source]

    out_ref[me] = lax.fori_loop(1, n, take, g_ref[me])

    def start2(d, _):
        gather(d).start()
        return 0

    lax.fori_loop(1, n, start2, 0)

    def finish(d, _):
        source = lax.rem(me + n - d, n)
        pltpu.make_async_remote_copy(
            src_ref=out_ref.at[source], dst_ref=out_ref.at[source], send_sem=s2.at[d], recv_sem=r2.at[d],
            device_id={"lines": source}, device_id_type=MESH).wait_recv()
        scatter(d).wait_send()
        gather(d).wait_send()
        return 0

    lax.fori_loop(1, n, finish, 0)


def whiten_kernel(info, g_ref, high_ref, low_ref, mat):
    h = g_ref.shape[1]
    bands = 2 * h
    total = (info[1] * info[2]).astype(F32)
    sums = jnp.concatenate([g_ref[3 * h : 3 * h + 8], g_ref[3 * h + 8 : 3 * h + 16]], axis=1)
    sums = jnp.where(iota((8, bands), 0) == 0, sums, 0.0)
    outer = lax.dot_general(sums, sums, TN, precision=HIGHEST, preferred_element_type=F32)
    scale = total - 1.0
    mat[:h, :h] = (g_ref[0:h] - outer[:h, :h] / total) / scale
    mat[:h, h:] = (g_ref[h : 2 * h] - outer[:h, h:] / total) / scale
    mat[h:, h:] = (g_ref[2 * h : 3 * h] - outer[h:, h:] / total) / scale
    mat[h:, :h] = jnp.zeros((h, h), F32)
    lane = iota((SLAB, bands), 1)
    row = iota((SLAB, bands), 0)
    for base in range(0, bands, SLAB):
        slab = mat[base : base + SLAB, :]
        pivots = jnp.ones((SLAB, bands), F32)
        for j in range(SLAB):
            k = base + j
            column = jnp.broadcast_to(slab[:, k : k + 1], (SLAB, bands))
            pivot = jnp.broadcast_to(column[j : j + 1, :], (SLAB, bands))
            pivots = jnp.where(row == j, pivot, pivots)
            factor = jnp.where(row > j, column / pivot, 0.0)
            line = jnp.broadcast_to(slab[j : j + 1, :], (SLAB, bands))
            line = jnp.where(lane == k, 1.0, line)
            slab = jnp.where((lane == k) & (row > j), 0.0, slab) - factor * line
        inside = (lane >= base) & (lane < base + SLAB)
        unit = jnp.where(lane == base + row, 1.0, jnp.where(inside & (lane > base + row), 0.0, slab))
        below = jnp.where(lane < base + SLAB, unit, 0.0)
        high, low = split(below * lax.rsqrt(pivots))
        high_ref[base : base + SLAB, :] = high
        low_ref[base : base + SLAB, :] = low
        rest = bands - base - SLAB
        if rest:
            update = lax.dot_general(
                slab, unit / pivots, TN, precision=HIGHEST, preferred_element_type=F32)
            old = mat[base + SLAB :, :]
            wide = iota((rest, bands), 1)
            cleared = jnp.where((wide >= base) & (wide < base + SLAB), 0.0, old)
            mat[base + SLAB :, :] = cleared - update[base + SLAB :, :]


def score_kernel(info, x_ref, before_ref, after_ref, high_ref, low_ref, out_ref, ext, outer, guard):
    lines, cols, bands = x_ref.shape
    first, last_line, last_col = info[0], info[1], info[2]
    col_ok = iota((cols, bands), 0) < last_col

    def mask(i, _):
        for part, ref in enumerate((before_ref, x_ref, after_ref)):
            line = first + (part - 1) * lines + i
            ok = col_ok & (line >= 0) & (line < last_line)
            ext[part * lines + i] = jnp.where(ok, ref[i].astype(F32), 0.0).astype(BF16)
        return 0

    lax.fori_loop(0, lines, mask, 0)

    def total(lo, hi):
        def add(i, acc):
            return acc + ext[i].astype(F32)
        return lax.fori_loop(lo, hi, add, jnp.zeros((cols, bands), F32))

    outer[...] = total(lines - OUTER, lines + OUTER)
    guard[...] = total(lines - GUARD, lines + GUARD)
    gap = jnp.abs(iota((cols, cols), 0) - iota((cols, cols), 1))
    near = jnp.where(gap <= OUTER, 1.0, 0.0).astype(BF16)
    close = jnp.where(gap <= GUARD, -1.0, 0.0).astype(BF16)
    windows = jnp.concatenate([near, near, close, close], axis=1)
    col = iota((cols, bands), 0)

    def span(place, end, radius):
        return jnp.maximum(jnp.minimum(place + radius, end - 1) - jnp.maximum(place - radius, 0) + 1, 0)

    outer_cols = span(col, last_col, OUTER).astype(F32)
    guard_cols = span(col, last_col, GUARD).astype(F32)
    step = 2

    def score(i, _):
        highs, lows = [], []
        for j in range(step):
            line = i * step + j
            at = lines + line
            wide = outer[...] + ext[at + OUTER].astype(F32)
            tight = guard[...] + ext[at + GUARD].astype(F32)
            stack = jnp.concatenate(split(wide) + split(tight), axis=0)
            outer[...] = wide - ext[at - OUTER].astype(F32)
            guard[...] = tight - ext[at - GUARD].astype(F32)
            cycle = jnp.dot(windows, stack, preferred_element_type=F32)
            place = first + line
            count = (span(place, last_line, OUTER).astype(F32) * outer_cols
                     - span(place, last_line, GUARD).astype(F32) * guard_cols)
            deviation = x_ref[line].astype(F32) - cycle / jnp.maximum(count, 1.0)
            high, low = split(deviation)
            highs.append(high)
            lows.append(low)
        high = jnp.concatenate(highs, axis=0)
        low = jnp.concatenate(lows, axis=0)
        white = lax.dot_general(high_ref[...], high, NT, preferred_element_type=F32)
        white += lax.dot_general(high_ref[...], low, NT, preferred_element_type=F32)
        white += lax.dot_general(low_ref[...], high, NT, preferred_element_type=F32)
        power = jnp.sum(white * white, axis=0, keepdims=True) / bands
        for j in range(step):
            line = i * step + j
            ok = (iota((1, cols), 1) < last_col) & (first + line < last_line)
            out_ref[pl.ds(line, 1), :] = jnp.where(ok, power[:, j * cols : (j + 1) * cols], 0.0)
        return 0

    lax.fori_loop(0, lines // step, score, 0)


VMEM = pl.BlockSpec(memory_space=pltpu.VMEM)
SMEM = pl.BlockSpec(memory_space=pltpu.SMEM)


def call(kernel, out_shape, specs, scratch, limit, flops, moved, **params):
    return pl.pallas_call(
        kernel, out_shape=out_shape, in_specs=specs,
        out_specs=jax.tree.map(lambda _: VMEM, out_shape), scratch_shapes=scratch,
        compiler_params=pltpu.CompilerParams(vmem_limit_bytes=limit << 20, **params),
        cost_estimate=pl.CostEstimate(flops=flops, bytes_accessed=moved, transcendentals=0))


def body(pixels, scene_lines, scene_cols):
    lines, cols, bands = pixels.shape
    n = lax.axis_size("lines")
    first = lax.axis_index("lines") * lines
    info = jnp.concatenate([first[None].astype(jnp.int32), scene_lines, scene_cols])
    half = bands // 2
    gram = call(
        gram_kernel, jax.ShapeDtypeStruct((4 * half, half), F32), [SMEM, VMEM],
        [pltpu.VMEM((bands, bands), F32), pltpu.VMEM((8, bands), F32)], 16,
        4000000000, pixels.size * 2)(info, pixels)
    gram = gram.reshape(n, 4 * half // n, half)
    sems = [pltpu.SemaphoreType.DMA((n,))] * 4
    gram = call(
        functools.partial(reduce_kernel, n), jax.ShapeDtypeStruct(gram.shape, F32), [VMEM],
        [pltpu.VMEM(gram.shape, F32)] + sems, 16, 4000000000, 40000000,
        collective_id=0, has_side_effects=True)(gram)
    gram, halo = lax.optimization_barrier((gram.reshape(4 * half, half), pixels))
    before = lax.ppermute(halo, "lines", [(i, i + 1) for i in range(n - 1)])
    after = lax.ppermute(halo, "lines", [(i + 1, i) for i in range(n - 1)])
    shape = jax.ShapeDtypeStruct((bands, bands), BF16)
    high, low = call(
        whiten_kernel, [shape, shape], [SMEM, VMEM], [pltpu.VMEM((bands, bands), F32)], 16,
        10000000000, 60000000)(info, gram)
    return call(
        score_kernel, jax.ShapeDtypeStruct((lines, cols), F32), [SMEM] + [VMEM] * 5,
        [pltpu.VMEM((lines + 2 * OUTER, cols, bands), BF16)] + [pltpu.VMEM((cols, bands), F32)] * 2, 40,
        8000000000, 8000000)(info, pixels, before, after, high, low)


def solution(mesh):
    in_specs = (P(("scene", "lines"), None, None), P("scene"), P("scene"))
    out_specs = P(("scene", "lines"), None)
    return jax.shard_map(body, mesh=mesh, in_specs=in_specs, out_specs=out_specs, check_vma=False)
```

```python
import functools

import jax
import jax.numpy as jnp
from jax import lax
from jax.experimental import pallas as pl
from jax.experimental.pallas import tpu as pltpu
from jax.sharding import PartitionSpec as P

OUTER = 32
GUARD = 4
SLAB = 32
GROUP = 8
EARLY = 8
HIGHEST = lax.Precision.HIGHEST
MESH = pl.DeviceIdType.MESH
BF16 = jnp.bfloat16
F32 = jnp.float32
TN = (((0,), (0,)), ((), ()))
NT = (((1,), (1,)), ((), ()))


def iota(shape, dim):
    return lax.broadcasted_iota(jnp.int32, shape, dim)


def split(value):
    high = value.astype(BF16)
    return high, (value - high.astype(F32)).astype(BF16)


def gram_kernel(info, x_ref, out_ref, gram, sums):
    lines, cols, bands = x_ref.shape
    first, last_line, last_col = info[0], info[1], info[2]
    col_ok = iota((cols, bands), 0) < last_col
    gram[...] = jnp.zeros_like(gram)
    sums[...] = jnp.zeros_like(sums)
    step = 4

    def add(i, _):
        rows = []
        for j in range(step):
            line = i * step + j
            ok = col_ok & (first + line < last_line)
            rows.append(jnp.where(ok, x_ref[line].astype(F32), 0.0).astype(BF16))
        block = jnp.concatenate(rows, axis=0)
        gram[...] += lax.dot_general(block, block, TN, preferred_element_type=F32)
        ones = jnp.ones((8, step * cols), BF16)
        sums[...] += jnp.dot(ones, block, preferred_element_type=F32)
        return 0

    lax.fori_loop(0, lines // step, add, 0)
    h = bands // 2
    out_ref[0:h] = gram[:h, :h]
    out_ref[h : 2 * h] = gram[:h, h:]
    out_ref[2 * h : 3 * h] = gram[h:, h:]
    out_ref[3 * h :] = jnp.zeros((h, h), F32)
    out_ref[3 * h : 3 * h + 8] = sums[:, :h]
    out_ref[3 * h + 8 : 3 * h + 16] = sums[:, h:]


def reduce_kernel(n, g_ref, out_ref, recv, s1, r1, s2, r2):
    me = lax.axis_index("lines")
    bar = pltpu.get_barrier_semaphore()

    def greet(d, _):
        pl.semaphore_signal(bar, inc=1, device_id={"lines": lax.rem(me + d, n)}, device_id_type=MESH)
        return 0

    lax.fori_loop(1, n, greet, 0)
    pl.semaphore_wait(bar, n - 1)

    def scatter(d):
        peer = lax.rem(me + d, n)
        return pltpu.make_async_remote_copy(
            src_ref=g_ref.at[peer], dst_ref=recv.at[me], send_sem=s1.at[d], recv_sem=r1.at[d],
            device_id={"lines": peer}, device_id_type=MESH)

    def gather(d):
        peer = lax.rem(me + d, n)
        return pltpu.make_async_remote_copy(
            src_ref=out_ref.at[me], dst_ref=out_ref.at[me], send_sem=s2.at[d], recv_sem=r2.at[d],
            device_id={"lines": peer}, device_id_type=MESH)

    def start1(d, _):
        scatter(d).start()
        return 0

    lax.fori_loop(1, n, start1, 0)

    def take(d, total):
        source = lax.rem(me + n - d, n)
        pltpu.make_async_remote_copy(
            src_ref=g_ref.at[source], dst_ref=recv.at[source], send_sem=s1.at[d], recv_sem=r1.at[d],
            device_id={"lines": source}, device_id_type=MESH).wait_recv()
        return total + recv[source]

    out_ref[me] = lax.fori_loop(1, n, take, g_ref[me])

    def start2(d, _):
        gather(d).start()
        return 0

    lax.fori_loop(1, n, start2, 0)

    def finish(d, _):
        source = lax.rem(me + n - d, n)
        pltpu.make_async_remote_copy(
            src_ref=out_ref.at[source], dst_ref=out_ref.at[source], send_sem=s2.at[d], recv_sem=r2.at[d],
            device_id={"lines": source}, device_id_type=MESH).wait_recv()
        scatter(d).wait_send()
        gather(d).wait_send()
        return 0

    lax.fori_loop(1, n, finish, 0)


def whiten_kernel(info, g_ref, high_ref, low_ref, mat):
    h = g_ref.shape[1]
    bands = 2 * h
    total = (info[1] * info[2]).astype(F32)
    sums = jnp.concatenate([g_ref[3 * h : 3 * h + 8], g_ref[3 * h + 8 : 3 * h + 16]], axis=1)
    sums = jnp.where(iota((8, bands), 0) == 0, sums, 0.0)
    outer = lax.dot_general(sums, sums, TN, precision=HIGHEST, preferred_element_type=F32)
    scale = total - 1.0
    mat[:h, :h] = (g_ref[0:h] - outer[:h, :h] / total) / scale
    mat[:h, h:] = (g_ref[h : 2 * h] - outer[:h, h:] / total) / scale
    mat[h:, h:] = (g_ref[2 * h : 3 * h] - outer[h:, h:] / total) / scale
    mat[h:, :h] = jnp.zeros((h, h), F32)
    lane = iota((SLAB, bands), 1)
    row = iota((SLAB, bands), 0)
    for base in range(0, bands, SLAB):
        slab = mat[base : base + SLAB, :]
        pivots = []
        for top in range(0, SLAB, GROUP):
            tail = slab[top:, :]
            size = SLAB - top
            narrow = iota((size, 128), 0)
            wide_row = iota((size, bands), 0)
            wide_lane = iota((size, bands), 1)
            columns = [
                jnp.broadcast_to(tail[:, k : k + 1], (size, 128))
                for k in range(base + top, base + top + GROUP)
            ]
            group = jnp.ones((GROUP, 128), F32)
            for j in range(GROUP):
                k = base + top + j
                pivot = jnp.broadcast_to(columns[j][j : j + 1, :], (GROUP, 128))
                group = jnp.where(iota((GROUP, 128), 0) == j, pivot, group)
                inverse = 1.0 / pivot
                inverse = jnp.concatenate([inverse] * (size // GROUP), axis=0)
                factor = jnp.where(narrow > j, columns[j] * inverse, 0.0)
                for m in range(j + 1, GROUP):
                    columns[m] = columns[m] - factor * jnp.broadcast_to(columns[m][j : j + 1, :], (size, 128))
                line = jnp.where(wide_lane[:1] == k, 1.0, tail[j : j + 1, :])
                keep = jnp.where((wide_lane == k) & (wide_row > j), 0.0, tail)
                spread = jnp.concatenate([factor] * (bands // 128), axis=1)
                tail = keep - spread * jnp.broadcast_to(line, (size, bands))
            slab = jnp.concatenate([slab[:top, :], tail], axis=0) if top else tail
            pivots.append(group)
        pivots = jnp.concatenate(pivots, axis=0)
        pivots = jnp.concatenate([pivots] * (bands // 128), axis=1)
        inside = (lane >= base) & (lane < base + SLAB)
        unit = jnp.where(lane == base + row, 1.0, jnp.where(inside & (lane > base + row), 0.0, slab))
        below = jnp.where(lane < base + SLAB, unit, 0.0)
        high, low = split(below * lax.rsqrt(pivots))
        high_ref[base : base + SLAB, :] = high
        low_ref[base : base + SLAB, :] = low
        rest = bands - base - SLAB
        if rest:
            update = lax.dot_general(
                slab, unit / pivots, TN, precision=HIGHEST, preferred_element_type=F32)
            old = mat[base + SLAB :, :]
            wide = iota((rest, bands), 1)
            cleared = jnp.where((wide >= base) & (wide < base + SLAB), 0.0, old)
            mat[base + SLAB :, :] = cleared - update[base + SLAB :, :]


def score_kernel(info, x_ref, before_far, before_near, after_near, after_far, high_ref, low_ref, out_ref, ext, outer, guard):
    lines, cols, bands = x_ref.shape
    first, last_line, last_col = info[0], info[1], info[2]
    col_ok = iota((cols, bands), 0) < last_col

    start = 0
    for ref in (before_far, before_near, x_ref, after_near, after_far):
        count = ref.shape[0]

        def mask(i, _, ref=ref, start=start):
            line = first - lines + start + i
            ok = col_ok & (line >= 0) & (line < last_line)
            ext[start + i] = jnp.where(ok, ref[i].astype(F32), 0.0).astype(BF16)
            return 0

        lax.fori_loop(0, count, mask, 0)
        start += count

    def total(lo, hi):
        def add(i, acc):
            return acc + ext[i].astype(F32)
        return lax.fori_loop(lo, hi, add, jnp.zeros((cols, bands), F32))

    outer[...] = total(lines - OUTER, lines + OUTER)
    guard[...] = total(lines - GUARD, lines + GUARD)
    gap = jnp.abs(iota((cols, cols), 0) - iota((cols, cols), 1))
    near = jnp.where(gap <= OUTER, 1.0, 0.0).astype(BF16)
    close = jnp.where(gap <= GUARD, -1.0, 0.0).astype(BF16)
    windows = jnp.concatenate([near, near, close, close], axis=1)
    col = iota((cols, bands), 0)

    def span(place, end, radius):
        return jnp.maximum(jnp.minimum(place + radius, end - 1) - jnp.maximum(place - radius, 0) + 1, 0)

    outer_cols = span(col, last_col, OUTER).astype(F32)
    guard_cols = span(col, last_col, GUARD).astype(F32)
    step = 2

    def score(i, _):
        highs, lows = [], []
        for j in range(step):
            line = i * step + j
            at = lines + line
            wide = outer[...] + ext[at + OUTER].astype(F32)
            tight = guard[...] + ext[at + GUARD].astype(F32)
            stack = jnp.concatenate(split(wide) + split(tight), axis=0)
            outer[...] = wide - ext[at - OUTER].astype(F32)
            guard[...] = tight - ext[at - GUARD].astype(F32)
            cycle = jnp.dot(windows, stack, preferred_element_type=F32)
            place = first + line
            count = (span(place, last_line, OUTER).astype(F32) * outer_cols
                     - span(place, last_line, GUARD).astype(F32) * guard_cols)
            deviation = x_ref[line].astype(F32) - cycle / jnp.maximum(count, 1.0)
            high, low = split(deviation)
            highs.append(high)
            lows.append(low)
        high = jnp.concatenate(highs, axis=0)
        low = jnp.concatenate(lows, axis=0)
        white = lax.dot_general(high_ref[...], high, NT, preferred_element_type=F32)
        white += lax.dot_general(high_ref[...], low, NT, preferred_element_type=F32)
        white += lax.dot_general(low_ref[...], high, NT, preferred_element_type=F32)
        power = jnp.sum(white * white, axis=0, keepdims=True) / bands
        for j in range(step):
            line = i * step + j
            ok = (iota((1, cols), 1) < last_col) & (first + line < last_line)
            out_ref[pl.ds(line, 1), :] = jnp.where(ok, power[:, j * cols : (j + 1) * cols], 0.0)
        return 0

    lax.fori_loop(0, lines // step, score, 0)


VMEM = pl.BlockSpec(memory_space=pltpu.VMEM)
SMEM = pl.BlockSpec(memory_space=pltpu.SMEM)


def call(kernel, out_shape, specs, scratch, limit, flops, moved, **params):
    return pl.pallas_call(
        kernel, out_shape=out_shape, in_specs=specs,
        out_specs=jax.tree.map(lambda _: VMEM, out_shape), scratch_shapes=scratch,
        compiler_params=pltpu.CompilerParams(vmem_limit_bytes=limit << 20, **params),
        cost_estimate=pl.CostEstimate(flops=flops, bytes_accessed=moved, transcendentals=0))


def body(pixels, scene_lines, scene_cols):
    lines, cols, bands = pixels.shape
    n = lax.axis_size("lines")
    first = lax.axis_index("lines") * lines
    info = jnp.concatenate([first[None].astype(jnp.int32), scene_lines, scene_cols])
    up = [(i, i + 1) for i in range(n - 1)]
    down = [(i + 1, i) for i in range(n - 1)]
    early_before = lax.ppermute(pixels[lines - EARLY :], "lines", up)
    early_after = lax.ppermute(pixels[:EARLY], "lines", down)
    half = bands // 2
    gram = call(
        gram_kernel, jax.ShapeDtypeStruct((4 * half, half), F32), [SMEM, VMEM],
        [pltpu.VMEM((bands, bands), F32), pltpu.VMEM((8, bands), F32)], 16,
        4000000000, pixels.size * 2)(info, pixels)
    gram = gram.reshape(n, 4 * half // n, half)
    sems = [pltpu.SemaphoreType.DMA((n,))] * 4
    gram = call(
        functools.partial(reduce_kernel, n), jax.ShapeDtypeStruct(gram.shape, F32), [VMEM],
        [pltpu.VMEM(gram.shape, F32)] + sems, 16, 4000000000, 40000000,
        collective_id=0, has_side_effects=True)(gram)
    gram, halo = lax.optimization_barrier((gram.reshape(4 * half, half), pixels))
    before = (lax.ppermute(halo[: lines - EARLY], "lines", up), early_before)
    after = (early_after, lax.ppermute(halo[EARLY:], "lines", down))
    shape = jax.ShapeDtypeStruct((bands, bands), BF16)
    high, low = call(
        whiten_kernel, [shape, shape], [SMEM, VMEM], [pltpu.VMEM((bands, bands), F32)], 16,
        10000000000, 60000000)(info, gram)
    return call(
        score_kernel, jax.ShapeDtypeStruct((lines, cols), F32), [SMEM] + [VMEM] * 7,
        [pltpu.VMEM((lines + 2 * OUTER, cols, bands), BF16)] + [pltpu.VMEM((cols, bands), F32)] * 2, 40,
        8000000000, 8000000)(info, pixels, *before, *after, high, low)


def solution(mesh):
    in_specs = (P(("scene", "lines"), None, None), P("scene"), P("scene"))
    out_specs = P(("scene", "lines"), None)
    return jax.shard_map(body, mesh=mesh, in_specs=in_specs, out_specs=out_specs, check_vma=False)
```

```python
import functools

import jax
import jax.numpy as jnp
from jax import lax
from jax.experimental import pallas as pl
from jax.experimental.pallas import tpu as pltpu
from jax.sharding import PartitionSpec as P

OUTER = 32
GUARD = 4
SLAB = 32
GROUP = 8
EARLY = 8
CHUNK = 4
HIGHEST = lax.Precision.HIGHEST
MESH = pl.DeviceIdType.MESH
BF16 = jnp.bfloat16
F32 = jnp.float32
TN = (((0,), (0,)), ((), ()))
NT = (((1,), (1,)), ((), ()))


def iota(shape, dim):
    return lax.broadcasted_iota(jnp.int32, shape, dim)


def split(value):
    high = value.astype(BF16)
    return high, (value - high.astype(F32)).astype(BF16)


def gram_kernel(info, x_ref, out_ref, gram, sums):
    lines, cols, bands = x_ref.shape
    first, last_line, last_col = info[0], info[1], info[2]
    col_ok = iota((cols, bands), 0) < last_col
    gram[...] = jnp.zeros_like(gram)
    sums[...] = jnp.zeros_like(sums)
    step = 4

    def add(i, _):
        rows = []
        for j in range(step):
            line = i * step + j
            ok = col_ok & (first + line < last_line)
            rows.append(jnp.where(ok, x_ref[line].astype(F32), 0.0).astype(BF16))
        block = jnp.concatenate(rows, axis=0)
        gram[...] += lax.dot_general(block, block, TN, preferred_element_type=F32)
        ones = jnp.ones((8, step * cols), BF16)
        sums[...] += jnp.dot(ones, block, preferred_element_type=F32)
        return 0

    lax.fori_loop(0, lines // step, add, 0)
    h = bands // 2
    out_ref[0:h] = gram[:h, :h]
    out_ref[h : 2 * h] = gram[:h, h:]
    out_ref[2 * h : 3 * h] = gram[h:, h:]
    out_ref[3 * h :] = jnp.zeros((h, h), F32)
    out_ref[3 * h : 3 * h + 8] = sums[:, :h]
    out_ref[3 * h + 8 : 3 * h + 16] = sums[:, h:]


def halo(source, target, send, recv, index, peer):
    return pltpu.make_async_remote_copy(
        src_ref=source, dst_ref=target, send_sem=send.at[index], recv_sem=recv.at[index],
        device_id={"lines": peer}, device_id_type=MESH)


def reduce_kernel(n, g_ref, x_ref, out_ref, before_ref, after_ref, recv, s1, r1, s2, r2, s3, r3):
    me = lax.axis_index("lines")
    lines = x_ref.shape[0]
    has_left, has_right = me > 0, me < n - 1
    left, right = lax.rem(me + n - 1, n), lax.rem(me + 1, n)
    near = x_ref.at[pl.ds(lines - EARLY, EARLY)]
    lead = x_ref.at[pl.ds(0, EARLY)]
    bar = pltpu.get_barrier_semaphore()

    def greet(d, _):
        pl.semaphore_signal(bar, inc=1, device_id={"lines": lax.rem(me + d, n)}, device_id_type=MESH)
        return 0

    lax.fori_loop(1, n, greet, 0)
    pl.semaphore_wait(bar, n - 1)

    def scatter(d):
        peer = lax.rem(me + d, n)
        return pltpu.make_async_remote_copy(
            src_ref=g_ref.at[peer], dst_ref=recv.at[me], send_sem=s1.at[d], recv_sem=r1.at[d],
            device_id={"lines": peer}, device_id_type=MESH)

    def gather(d):
        peer = lax.rem(me + d, n)
        return pltpu.make_async_remote_copy(
            src_ref=out_ref.at[me], dst_ref=out_ref.at[me], send_sem=s2.at[d], recv_sem=r2.at[d],
            device_id={"lines": peer}, device_id_type=MESH)

    def start1(d, _):
        scatter(d).start()
        return 0

    lax.fori_loop(1, n, start1, 0)

    @pl.when(has_right)
    def _():
        halo(near, before_ref, s3, r3, 0, right).start()

    @pl.when(has_left)
    def _():
        halo(lead, after_ref, s3, r3, 1, left).start()

    def take(d, total):
        source = lax.rem(me + n - d, n)
        pltpu.make_async_remote_copy(
            src_ref=g_ref.at[source], dst_ref=recv.at[source], send_sem=s1.at[d], recv_sem=r1.at[d],
            device_id={"lines": source}, device_id_type=MESH).wait_recv()
        return total + recv[source]

    out_ref[me] = lax.fori_loop(1, n, take, g_ref[me])

    def start2(d, _):
        gather(d).start()
        return 0

    lax.fori_loop(1, n, start2, 0)

    def finish(d, _):
        source = lax.rem(me + n - d, n)
        pltpu.make_async_remote_copy(
            src_ref=out_ref.at[source], dst_ref=out_ref.at[source], send_sem=s2.at[d], recv_sem=r2.at[d],
            device_id={"lines": source}, device_id_type=MESH).wait_recv()
        scatter(d).wait_send()
        gather(d).wait_send()
        return 0

    lax.fori_loop(1, n, finish, 0)

    @pl.when(has_right)
    def _():
        halo(near, before_ref, s3, r3, 0, right).wait_send()
        halo(lead, after_ref, s3, r3, 1, right).wait_recv()

    @pl.when(has_left)
    def _():
        halo(lead, after_ref, s3, r3, 1, left).wait_send()
        halo(near, before_ref, s3, r3, 0, left).wait_recv()


def whiten_part(info, g_ref, high_ref, low_ref, mat):
    h = g_ref.shape[1]
    bands = 2 * h
    total = (info[1] * info[2]).astype(F32)
    sums = jnp.concatenate([g_ref[3 * h : 3 * h + 8], g_ref[3 * h + 8 : 3 * h + 16]], axis=1)
    sums = jnp.where(iota((8, bands), 0) == 0, sums, 0.0)
    outer = lax.dot_general(sums, sums, TN, precision=HIGHEST, preferred_element_type=F32)
    scale = total - 1.0
    mat[:h, :h] = (g_ref[0:h] - outer[:h, :h] / total) / scale
    mat[:h, h:] = (g_ref[h : 2 * h] - outer[:h, h:] / total) / scale
    mat[h:, h:] = (g_ref[2 * h : 3 * h] - outer[h:, h:] / total) / scale
    mat[h:, :h] = jnp.zeros((h, h), F32)
    lane = iota((SLAB, bands), 1)
    row = iota((SLAB, bands), 0)
    for base in range(0, bands, SLAB):
        slab = mat[base : base + SLAB, :]
        pivots = []
        for top in range(0, SLAB, GROUP):
            tail = slab[top:, :]
            size = SLAB - top
            narrow = iota((size, 128), 0)
            wide_row = iota((size, bands), 0)
            wide_lane = iota((size, bands), 1)
            columns = [
                jnp.broadcast_to(tail[:, k : k + 1], (size, 128))
                for k in range(base + top, base + top + GROUP)
            ]
            group = jnp.ones((GROUP, 128), F32)
            for j in range(GROUP):
                k = base + top + j
                pivot = jnp.broadcast_to(columns[j][j : j + 1, :], (GROUP, 128))
                group = jnp.where(iota((GROUP, 128), 0) == j, pivot, group)
                inverse = 1.0 / pivot
                inverse = jnp.concatenate([inverse] * (size // GROUP), axis=0)
                factor = jnp.where(narrow > j, columns[j] * inverse, 0.0)
                for m in range(j + 1, GROUP):
                    columns[m] = columns[m] - factor * jnp.broadcast_to(columns[m][j : j + 1, :], (size, 128))
                line = jnp.where(wide_lane[:1] == k, 1.0, tail[j : j + 1, :])
                keep = jnp.where((wide_lane == k) & (wide_row > j), 0.0, tail)
                spread = jnp.concatenate([factor] * (bands // 128), axis=1)
                tail = keep - spread * jnp.broadcast_to(line, (size, bands))
            slab = jnp.concatenate([slab[:top, :], tail], axis=0) if top else tail
            pivots.append(group)
        pivots = jnp.concatenate(pivots, axis=0)
        pivots = jnp.concatenate([pivots] * (bands // 128), axis=1)
        inside = (lane >= base) & (lane < base + SLAB)
        unit = jnp.where(lane == base + row, 1.0, jnp.where(inside & (lane > base + row), 0.0, slab))
        below = jnp.where(lane < base + SLAB, unit, 0.0)
        high, low = split(below * lax.rsqrt(pivots))
        high_ref[base : base + SLAB, :] = high
        low_ref[base : base + SLAB, :] = low
        rest = bands - base - SLAB
        if rest:
            update = lax.dot_general(
                slab, unit / pivots, TN, precision=HIGHEST, preferred_element_type=F32)
            old = mat[base + SLAB :, :]
            wide = iota((rest, bands), 1)
            cleared = jnp.where((wide >= base) & (wide < base + SLAB), 0.0, old)
            mat[base + SLAB :, :] = cleared - update[base + SLAB :, :]


def score_kernel(n, info, g_ref, x_ref, near_before, near_after, out_ref, far_before, far_after,
                 high_ref, low_ref, mat, ext, outer_f, guard_f, outer_b, guard_b, send, recv):
    lines, cols, bands = x_ref.shape
    far = lines - EARLY
    chunks = far // CHUNK
    me = lax.axis_index("lines")
    has_left, has_right = me > 0, me < n - 1
    left, right = lax.rem(me + n - 1, n), lax.rem(me + 1, n)
    bar = pltpu.get_barrier_semaphore()

    @pl.when(has_left)
    def _():
        pl.semaphore_signal(bar, inc=1, device_id={"lines": left}, device_id_type=MESH)

    @pl.when(has_right)
    def _():
        pl.semaphore_signal(bar, inc=1, device_id={"lines": right}, device_id_type=MESH)

    pl.semaphore_wait(bar, has_left.astype(jnp.int32) + has_right.astype(jnp.int32))

    def copy_before(m, peer):
        rows = pl.ds(far - (m + 1) * CHUNK, CHUNK)
        return halo(x_ref.at[rows], far_before.at[rows], send, recv, m, peer)

    def copy_after(m, peer):
        return halo(x_ref.at[pl.ds(EARLY + m * CHUNK, CHUNK)], far_after.at[pl.ds(m * CHUNK, CHUNK)],
                    send, recv, chunks + m, peer)

    for m in range(chunks):
        @pl.when(has_right)
        def _():
            copy_before(m, right).start()

        @pl.when(has_left)
        def _():
            copy_after(m, left).start()

    whiten_part(info, g_ref, high_ref, low_ref, mat)

    first, last_line, last_col = info[0], info[1], info[2]
    col_ok = iota((cols, bands), 0) < last_col

    def mask(ref, source, start, count):
        def one(i, _):
            line = first - lines + start + i
            ok = col_ok & (line >= 0) & (line < last_line)
            ext[start + i] = jnp.where(ok, ref[source + i].astype(F32), 0.0).astype(BF16)
            return 0
        lax.fori_loop(0, count, one, 0)

    mask(near_before, 0, far, EARLY)
    mask(x_ref, 0, lines, lines)
    mask(near_after, 0, 2 * lines, EARLY)

    def total(lo, hi, acc):
        def add(i, acc):
            return acc + ext[i].astype(F32)
        return lax.fori_loop(lo, hi, add, acc)

    half = lines // 2
    zero = jnp.zeros((cols, bands), F32)
    guard_f[...] = total(lines + half - GUARD, lines + half + GUARD, zero)
    guard_b[...] = guard_f[...]
    outer_f[...] = total(far, 2 * lines + EARLY, zero)

    gap = jnp.abs(iota((cols, cols), 0) - iota((cols, cols), 1))
    near = jnp.where(gap <= OUTER, 1.0, 0.0).astype(BF16)
    close = jnp.where(gap <= GUARD, -1.0, 0.0).astype(BF16)
    windows = jnp.concatenate([near, near, close, close], axis=1)
    col = iota((cols, bands), 0)

    def span(place, end, radius):
        return jnp.maximum(jnp.minimum(place + radius, end - 1) - jnp.maximum(place - radius, 0) + 1, 0)

    outer_cols = span(col, last_col, OUTER).astype(F32)
    guard_cols = span(col, last_col, GUARD).astype(F32)

    def deviate(line, wide, tight):
        stack = jnp.concatenate(split(wide) + split(tight), axis=0)
        cycle = jnp.dot(windows, stack, preferred_element_type=F32)
        place = first + line
        count = (span(place, last_line, OUTER).astype(F32) * outer_cols
                 - span(place, last_line, GUARD).astype(F32) * guard_cols)
        return split(x_ref[line].astype(F32) - cycle / jnp.maximum(count, 1.0))

    def score(base):
        def one(i, _):
            places, parts = [], []
            for j in range(2):
                line = half + base + i * 2 + j
                at = lines + line
                wide = outer_f[...] + ext[at + OUTER].astype(F32)
                tight = guard_f[...] + ext[at + GUARD].astype(F32)
                outer_f[...] = wide - ext[at - OUTER].astype(F32)
                guard_f[...] = tight - ext[at - GUARD].astype(F32)
                places.append(line)
                parts.append(deviate(line, wide, tight))
                line = half - 1 - base - i * 2 - j
                at = lines + line
                wide = outer_b[...] + ext[at - OUTER].astype(F32)
                tight = guard_b[...] + ext[at - GUARD].astype(F32)
                outer_b[...] = wide - ext[at + OUTER].astype(F32)
                guard_b[...] = tight - ext[at + GUARD].astype(F32)
                places.append(line)
                parts.append(deviate(line, wide, tight))
            high = jnp.concatenate([p[0] for p in parts], axis=0)
            low = jnp.concatenate([p[1] for p in parts], axis=0)
            white = lax.dot_general(high_ref[...], high, NT, preferred_element_type=F32)
            white += lax.dot_general(high_ref[...], low, NT, preferred_element_type=F32)
            white += lax.dot_general(low_ref[...], high, NT, preferred_element_type=F32)
            power = jnp.sum(white * white, axis=0, keepdims=True) / bands
            for j, line in enumerate(places):
                ok = (iota((1, cols), 1) < last_col) & (first + line < last_line)
                out_ref[pl.ds(line, 1), :] = jnp.where(ok, power[:, j * cols : (j + 1) * cols], 0.0)
            return 0
        lax.fori_loop(0, CHUNK // 2, one, 0)

    ready = (half - EARLY) // CHUNK
    for m in range(chunks):
        @pl.when(has_left)
        def _():
            copy_before(m, left).wait_recv()

        @pl.when(has_right)
        def _():
            copy_after(m, right).wait_recv()

        lo = far - (m + 1) * CHUNK
        hi = m * CHUNK
        mask(far_before, lo, lo, CHUNK)
        mask(far_after, hi, 2 * lines + EARLY + hi, CHUNK)
        if m < ready:
            acc = total(lo, lo + CHUNK, outer_f[...])
            outer_f[...] = total(2 * lines + EARLY + hi, 2 * lines + EARLY + hi + CHUNK, acc)
            if m == ready - 1:
                outer_b[...] = outer_f[...]
        else:
            score((m - ready) * CHUNK)

    for m in range(chunks):
        @pl.when(has_right)
        def _():
            copy_before(m, right).wait_send()

        @pl.when(has_left)
        def _():
            copy_after(m, left).wait_send()


VMEM = pl.BlockSpec(memory_space=pltpu.VMEM)
SMEM = pl.BlockSpec(memory_space=pltpu.SMEM)


def call(kernel, out_shape, specs, scratch, limit, flops, moved, **params):
    return pl.pallas_call(
        kernel, out_shape=out_shape, in_specs=specs,
        out_specs=jax.tree.map(lambda _: VMEM, out_shape), scratch_shapes=scratch,
        compiler_params=pltpu.CompilerParams(vmem_limit_bytes=limit << 20, **params),
        cost_estimate=pl.CostEstimate(flops=flops, bytes_accessed=moved, transcendentals=0))


def body(pixels, scene_lines, scene_cols):
    lines, cols, bands = pixels.shape
    n = lax.axis_size("lines")
    first = lax.axis_index("lines") * lines
    info = jnp.concatenate([first[None].astype(jnp.int32), scene_lines, scene_cols])
    half = bands // 2
    gram = call(
        gram_kernel, jax.ShapeDtypeStruct((4 * half, half), F32), [SMEM, VMEM],
        [pltpu.VMEM((bands, bands), F32), pltpu.VMEM((8, bands), F32)], 16,
        4000000000, pixels.size * 2)(info, pixels)
    gram = gram.reshape(n, 4 * half // n, half)
    sems = [pltpu.SemaphoreType.DMA((n,))] * 4
    edge = jax.ShapeDtypeStruct((EARLY, cols, bands), BF16)
    gram, before, after = call(
        functools.partial(reduce_kernel, n), [jax.ShapeDtypeStruct(gram.shape, F32), edge, edge], [VMEM, VMEM],
        [pltpu.VMEM(gram.shape, F32)] + sems + [pltpu.SemaphoreType.DMA((2,))] * 2, 32, 4000000000, 40000000,
        collective_id=0, has_side_effects=True)(gram, pixels)
    gram = gram.reshape(4 * half, half)
    far = lines - EARLY
    pieces = pltpu.SemaphoreType.DMA((2 * (far // CHUNK),))
    scratch = (
        [pltpu.VMEM((far, cols, bands), BF16)] * 2 + [pltpu.VMEM((bands, bands), BF16)] * 2
        + [pltpu.VMEM((bands, bands), F32), pltpu.VMEM((lines + 2 * OUTER, cols, bands), BF16)]
        + [pltpu.VMEM((cols, bands), F32)] * 4 + [pieces] * 2)
    return call(
        functools.partial(score_kernel, n), jax.ShapeDtypeStruct((lines, cols), F32), [SMEM] + [VMEM] * 4,
        scratch, 48, 8000000000, 80000000, collective_id=1, has_side_effects=True)(
            info, gram, pixels, before, after)


def solution(mesh):
    in_specs = (P(("scene", "lines"), None, None), P("scene"), P("scene"))
    out_specs = P(("scene", "lines"), None)
    return jax.shard_map(body, mesh=mesh, in_specs=in_specs, out_specs=out_specs, check_vma=False)
```
